32 devices in a mesh: dp: 8 (over z, x), tensor: 4 (over y, core).
Axes of the slice: x: 2, y: 2, z: 4, core: 2. Of those that a mesh axis runs over, the one named last changes fastest.
Arguments:
- tokens: bfloat16 [8192, 2048], P('dp'), may hold values from -6 to 6
- out_grad: bfloat16 [8192, 2048], P('dp'), may hold values from -6 to 6
- starts: int32 [5], replicated, may hold values from 0 to 7936, as said below
- attn_gain: bfloat16 [2048], P('dp'), may hold values from 0.5 to 1.5
- w_query: bfloat16 [2048, 1024], P('dp', 'tensor'), may hold values from -0.125 to 0.125
- w_key: bfloat16 [2048, 1024], P('dp', 'tensor'), may hold values from -0.125 to 0.125
- w_value: bfloat16 [2048, 2048], P('dp', 'tensor'), may hold values from -0.125 to 0.125
- w_outgate: bfloat16 [2048, 2048], P('dp', 'tensor'), may hold values from -0.125 to 0.125
- w_decay_down: bfloat16 [2048, 16], P('dp'), may hold values from -0.125 to 0.125
- w_decay_up: bfloat16 [16, 1024], P(None, ('tensor', 'dp')), may hold values from -1.5 to 1.5
- decay_bias: bfloat16 [1024], P(('tensor', 'dp')), may hold values from -1 to 10
- head_gain: bfloat16 [2048], P(('tensor', 'dp')), may hold values from 0.5 to 1.5
- w_output: bfloat16 [2048, 2048], P('tensor', 'dp'), may hold values from -0.25 to 0.25
- ffn_gain: bfloat16 [2048], P('dp'), may hold values from 0.5 to 1.5
- w_gate: bfloat16 [2048, 5632], P('dp', 'tensor'), may hold values from -0.125 to 0.125
- w_up: bfloat16 [2048, 5632], P('dp', 'tensor'), may hold values from -0.125 to 0.125
- w_down: bfloat16 [5632, 2048], P('tensor', 'dp'), may hold values from -0.21875 to 0.21875
Outputs:
- output: bfloat16 [8192, 2048], P('dp')
- input_grad: float32 [8192, 2048], P('dp')
- grad_attn_gain: float32 [2048], P('dp')
- grad_w_query: float32 [2048, 1024], P('dp', 'tensor')
- grad_w_key: float32 [2048, 1024], P('dp', 'tensor')
- grad_w_value: float32 [2048, 2048], P('dp', 'tensor')
- grad_w_outgate: float32 [2048, 2048], P('dp', 'tensor')
- grad_w_decay_down: float32 [2048, 16], P('dp')
- grad_w_decay_up: float32 [16, 1024], P(None, ('tensor', 'dp'))
- grad_decay_bias: float32 [1024], P(('tensor', 'dp'))
- grad_head_gain: float32 [2048], P(('tensor', 'dp'))
- grad_w_output: float32 [2048, 2048], P('tensor', 'dp')
- grad_ffn_gain: float32 [2048], P('dp')
- grad_w_gate: float32 [2048, 5632], P('dp', 'tensor')
- grad_w_up: float32 [2048, 5632], P('dp', 'tensor')
- grad_w_down: float32 [5632, 2048], P('tensor', 'dp')
The draws below stay inside these ranges and needn't reach their ends.
Inputs may be any that keep to these rules, and one draw needn't show every extreme that they name: `starts`: strictly increasing, the first is 0; the last is 7936.
All inputs are finite; a program needn't handle non-finite values.
Results may differ from the reference program's by a relative error of at most 0.018.
Values may be sent and summed in bfloat16 or wider, within the bound.
No kernel may reach another device: no remote copies, remote signals or barrier semaphores. Data moves between devices by JAX's collectives and lax.ppermute only.
A program may use at most 256 MiB of HBM per device.

```python
import jax
import jax.numpy as jnp
from jax import lax

D = 2048
HEADS = 4
DK = 256
DV = 512
FF = 5632
RANK = 16
GROUP = 64
TOK_DEV = 1024
TOKENS = 8192
KD = 1024
VD = 2048


def draw_starts(key, part):
    key = jax.random.fold_in(key, 11)
    first_key, second_key, third_key = jax.random.split(key, 3)
    halfway = TOK_DEV // 2
    second = jax.random.randint(first_key, (), 1, halfway)
    third = jax.random.randint(second_key, (), halfway, TOK_DEV)
    fourth = TOKENS - TOK_DEV + jax.random.randint(third_key, (), 1, halfway)
    fifth = jnp.full((), TOKENS - TOK_DEV // 4, jnp.int32)
    return jnp.stack([jnp.zeros((), jnp.int32), second, third, fourth, fifth]).astype(jnp.int32)


def steps_of(stream_key, shape, pieces, least, high):
    def one(position, blocks):
        steps = jax.random.uniform(jax.random.fold_in(jax.random.fold_in(stream_key, 6), position), (blocks,), jnp.float32, least / len(pieces), high / len(pieces))
        return jnp.repeat(jnp.exp(steps), shape[position] // blocks).reshape((-1,) + (1,) * (len(shape) - position - 1))

    loudness = one(*pieces[0])
    for cut in pieces[1:]:
        loudness = loudness * one(*cut)
    return loudness


def normal_values(stream_key, extent, spread, reach, pieces=(), kind=jnp.bfloat16):
    array = jax.random.normal(stream_key, extent, jnp.float32) * spread
    if len(pieces) > 0:
        array = steps_of(stream_key, extent, pieces, -0.22, 0.18) * array
    return jnp.clip(array, min=-reach, max=reach).astype(kind)


def setup_inputs(seed: int = 0) -> dict:
    key_list = jax.random.split(jax.random.key(seed), 18)
    tokens = normal_values(key_list[0], (TOKENS, D), 1.0, 6.0, ((0, 8),))
    out_grad = normal_values(key_list[1], (TOKENS, D), 1.0, 6.0, ((0, 8),))
    starts = draw_starts(jax.random.fold_in(key_list[17], 71), 0)
    attn_gain = jnp.clip(1.0 + 0.1 * jax.random.normal(key_list[3], (D,), jnp.float32), 0.5, 1.5).astype(jnp.bfloat16)
    w_query = normal_values(key_list[4], (D, KD), D ** -0.5, 0.125, ((0, 8), (1, 4)))
    w_key = normal_values(key_list[5], (D, KD), D ** -0.5, 0.125, ((0, 8), (1, 4)))
    w_value = normal_values(key_list[6], (D, VD), D ** -0.5, 0.125, ((0, 8), (1, 4)))
    w_outgate = normal_values(key_list[7], (D, VD), D ** -0.5, 0.125, ((0, 8), (1, 4)))
    w_decay_down = normal_values(key_list[8], (D, RANK), D ** -0.5, 0.125, ((0, 8),))
    w_decay_up = normal_values(key_list[9], (RANK, KD), RANK ** -0.5, 1.5, ((1, 32),))
    decay_bias = jnp.clip(-1.0 + 11.0 * jax.random.uniform(key_list[10], (KD,), jnp.float32) ** steps_of(key_list[10], (KD,), ((0, 32),), -0.2, 0.2), -1.0, 10.0).astype(jnp.bfloat16)
    head_gain = jnp.clip(1.0 + 0.1 * jax.random.normal(key_list[11], (VD,), jnp.float32), 0.5, 1.5).astype(jnp.bfloat16)
    w_output = normal_values(key_list[12], (VD, D), (D // 4) ** -0.5, 0.25, ((0, 4), (1, 8)))
    ffn_gain = jnp.clip(1.0 + 0.1 * jax.random.normal(key_list[13], (D,), jnp.float32), 0.5, 1.5).astype(jnp.bfloat16)
    w_gate = normal_values(key_list[14], (D, FF), D ** -0.5, 0.125, ((0, 8), (1, 4)))
    w_up = normal_values(key_list[15], (D, FF), D ** -0.5, 0.125, ((0, 8), (1, 4)))
    w_down = normal_values(key_list[16], (FF, D), (FF // 8) ** -0.5, 0.21875, ((0, 4), (1, 8)))
    return dict(tokens=tokens, out_grad=out_grad, starts=starts, attn_gain=attn_gain, w_query=w_query, w_key=w_key, w_value=w_value, w_outgate=w_outgate, w_decay_down=w_decay_down, w_decay_up=w_decay_up, decay_bias=decay_bias, head_gain=head_gain, w_output=w_output, ffn_gain=ffn_gain, w_gate=w_gate, w_up=w_up, w_down=w_down)


@jax.custom_vjp
def low(v):
    return lax.optimization_barrier(v.astype(jnp.bfloat16)).astype(jnp.float32)

@jax.custom_vjp
def low_back(v):
    return v

def low_keep(v):
    return (low(v), None)

def low_pass(kept, grad):
    return (grad,)

def back_keep(v):
    return (v, None)

def back_low(kept, grad):
    return (low(grad),)
low.defvjp(low_keep, low_pass)
low_back.defvjp(back_keep, back_low)
HIGHEST_PRECISION = lax.Precision.HIGHEST
EPSILON = 1e-06
GATE_NORMALIZER = 16.0

def matmul(left, right):
    return jnp.dot(left, right, precision=HIGHEST_PRECISION)

def rms_scale(values, gains):
    return values * lax.rsqrt(lax.optimization_barrier(jnp.mean(values * values, axis=-1, keepdims=True)) + EPSILON) * gains

def group_step(carried, inputs):
    block_q, block_k, block_v, block_decay, block_segment, segment_prev = inputs
    cumulative = jnp.cumsum(block_decay, axis=0)
    q_scaled = block_q * jnp.exp(cumulative)
    k_scaled = block_k * jnp.exp(-cumulative)
    scores = jnp.einsum('thc,shc->hts', q_scaled, k_scaled, precision=HIGHEST_PRECISION)
    length = block_q.shape[0]
    places = jnp.arange(length)
    allowed = (places[None, :] <= places[:, None]) & (block_segment[None, :] == block_segment[:, None])
    scores = jnp.where(allowed[None], scores, 0.0)
    within = jnp.einsum('hts,shv->thv', scores, block_v, precision=HIGHEST_PRECISION)
    carry_on = (block_segment == segment_prev).astype(jnp.float32)
    outside = jnp.einsum('thc,hcv->thv', q_scaled, carried, precision=HIGHEST_PRECISION) * carry_on[:, None, None]
    at_end = cumulative[-1]
    same_last = (block_segment == block_segment[-1]).astype(jnp.float32)
    k_end = block_k * jnp.exp(at_end[None] - cumulative) * same_last[:, None, None]
    updated = carried * (jnp.exp(at_end) * carry_on[-1])[:, :, None]
    updated = updated + jnp.einsum('shc,shv->hcv', k_end, block_v, precision=HIGHEST_PRECISION)
    return (updated, within + outside)

def gla_stream(queries, keys_in, values, log_decay, segment):
    count = queries.shape[0]
    blocks = count // GROUP
    previous = jnp.concatenate([jnp.full((1,), -1, jnp.int32), segment[:-1]])[::GROUP]
    initial = jnp.zeros((HEADS, DK, DV), jnp.float32)
    inputs = (queries.reshape(blocks, GROUP, HEADS, DK), keys_in.reshape(blocks, GROUP, HEADS, DK), values.reshape(blocks, GROUP, HEADS, DV), log_decay.reshape(blocks, GROUP, HEADS, DK), segment.reshape(blocks, GROUP), previous)
    finished, outputs = lax.scan(jax.checkpoint(group_step), initial, inputs)
    return outputs.reshape(count, HEADS, DV)

def block(inputs, params, segment):
    attn_gain, w_query, w_key, w_value, w_outgate, w_decay_down, w_decay_up, decay_bias, head_gain, w_output, ffn_gain, w_gate, w_up, w_down = params
    count = inputs.shape[0]
    normed = low(rms_scale(inputs, attn_gain))
    queries = low_back(matmul(normed, w_query))
    keys_in = low_back(matmul(normed, w_key))
    values = low_back(matmul(normed, w_value))
    outgate = low_back(matmul(normed, w_outgate))
    decay_low = low_back(matmul(normed, w_decay_down))
    decay_logit = matmul(decay_low, w_decay_up) + decay_bias
    log_decay = jax.nn.log_sigmoid(decay_logit) / GATE_NORMALIZER
    mixed = gla_stream((queries * DK ** (-0.5)).reshape(count, HEADS, DK), keys_in.reshape(count, HEADS, DK), values.reshape(count, HEADS, DV), log_decay.reshape(count, HEADS, DK), segment)
    head_out = rms_scale(mixed, head_gain.reshape(HEADS, DV))
    gated = low((head_out * jax.nn.silu(outgate.reshape(count, HEADS, DV))).reshape(count, HEADS * DV))
    branch = low_back(matmul(gated, w_output))
    hidden_in = inputs + branch
    normed_two = low(rms_scale(hidden_in, ffn_gain))
    gate_pre = low_back(matmul(normed_two, w_gate))
    up_proj = low_back(matmul(normed_two, w_up))
    hidden = low(jax.nn.silu(gate_pre) * up_proj)
    return hidden_in + low_back(matmul(hidden, w_down))

def reference(tokens, out_grad, starts, attn_gain, w_query, w_key, w_value, w_outgate, w_decay_down, w_decay_up, decay_bias, head_gain, w_output, ffn_gain, w_gate, w_up, w_down):
    positions = jnp.arange(tokens.shape[0]).astype(jnp.int32)
    segment = (lax.optimization_barrier(jnp.sum((starts[None, :] <= positions[:, None]).astype(jnp.int32), axis=1)) - 1).astype(jnp.int32)
    weights = tuple((item.astype(jnp.float32) for item in (attn_gain, w_query, w_key, w_value, w_outgate, w_decay_down, w_decay_up, decay_bias, head_gain, w_output, ffn_gain, w_gate, w_up, w_down)))

    def forward(inputs, *params):
        return block(inputs, params, segment)
    result, pullback = jax.vjp(forward, tokens.astype(jnp.float32), *weights)
    grads = pullback(out_grad.astype(jnp.float32))
    return (result.astype(jnp.bfloat16), grads[0], grads[1], grads[2], grads[3], grads[4], grads[5], grads[6], grads[7], grads[8], grads[9], grads[10], grads[11], grads[12], grads[13], grads[14])
```

```python
import functools

import jax
import jax.numpy as jnp
from jax import lax
from jax.experimental import pallas as pl
from jax.experimental.pallas import tpu as pltpu
from jax.sharding import PartitionSpec as P

DK = 256
DV = 512
RANK = 16
BLOCK = 128
SMALL = 128
EPSILON = 1e-06
GATE_NORMALIZER = 16.0
HIGHEST = lax.Precision.HIGHEST
F32 = jnp.float32
BF16 = jnp.bfloat16
NN = ((1,), (0,))
NT = ((1,), (1,))
TN = ((0,), (0,))
VMEM_BYTES = 50 * 1024 * 1024


def low_dot(left, right, dims):
    return lax.dot_general(
        left.astype(BF16), right.astype(BF16), (dims, ((), ())), preferred_element_type=F32
    )


class Ring:
    def __init__(self, axis, depth=2):
        self.axis, self.depth = axis, depth
        self.n = lax.axis_size(axis)
        n = self.n
        order = list(range(0, n, 2)) + list(range(n - 1, 0, -2))
        self.nexts = [(order[i], order[(i + 1) % n]) for i in range(n)]
        self.prevs = [(order[i], order[(i - 1) % n]) for i in range(n)]
        me = lax.axis_index(axis)
        self.place = jnp.where(me % 2 == 0, me // 2, n - 1 - me // 2)
        self.sent = ([], [])

    def at(self, offset):
        place = (self.place + offset + self.n) % self.n
        return jnp.where(place < self.n // 2, 2 * place, 2 * (self.n - place) - 1)

    def send(self, value, backward):
        past = self.sent[backward]
        if len(past) >= self.depth:
            value, _ = lax.optimization_barrier((value, past[-self.depth]))
        arrived = lax.ppermute(value, self.axis, self.prevs if backward else self.nexts)
        past.append(arrived)
        return arrived

    def gather(self, parts, dims):
        n = self.n

        def put(whole, piece, block, dim, extra=0):
            start = [0, 0]
            start[dim] = block * part_size[dim] + (extra if dim == 0 else 0)
            if dim == 1:
                start[0] = extra
            return lax.dynamic_update_slice(whole, piece, start)

        wholes = []
        for part, dim in zip(parts, dims):
            part_size = part.shape
            shape = list(part.shape)
            shape[dim] *= n
            wholes.append(put(jnp.zeros(shape, part.dtype), part, self.at(0), dim))
        ahead, behind = list(parts), list(parts)
        for step in range(1, n // 2):
            for i, dim in enumerate(dims):
                part_size = parts[i].shape
                ahead[i] = self.send(ahead[i], 0)
                behind[i] = self.send(behind[i], 1)
                wholes[i] = put(wholes[i], ahead[i], self.at(-step), dim)
                wholes[i] = put(wholes[i], behind[i], self.at(step), dim)
        for i, dim in enumerate(dims):
            part_size = parts[i].shape
            half = part_size[0] // 2
            first = self.send(ahead[i][:half], 0)
            second = self.send(behind[i][half:], 1)
            far = self.at(n // 2)
            wholes[i] = put(wholes[i], first, far, dim)
            wholes[i] = put(wholes[i], second, far, dim, half)
        return wholes

    def scatter(self, makers):
        n = self.n
        ahead, behind = [], []
        for maker in makers:
            far = maker(self.at(n // 2)).astype(BF16)
            half = far.shape[0] // 2
            ahead.append(self.send(far[:half], 0))
            behind.append(self.send(far[half:], 1))
        for step in range(n // 2 - 1, 0, -1):
            for i, maker in enumerate(makers):
                front, back = maker(self.at(step)), maker(self.at(-step))
                came, went = ahead[i].astype(F32), behind[i].astype(F32)
                if step == n // 2 - 1:
                    rest = front.shape[0] - came.shape[0]
                    came = jnp.pad(came, ((0, rest), (0, 0)))
                    went = jnp.pad(went, ((front.shape[0] - went.shape[0], 0), (0, 0)))
                ahead[i] = self.send((front + came).astype(BF16), 0)
                behind[i] = self.send((back + went).astype(BF16), 1)
        return [
            maker(self.at(0)) + ahead[i].astype(F32) + behind[i].astype(F32)
            for i, maker in enumerate(makers)
        ]


def swap(value, distance):
    return lax.ppermute(value, "tensor", [(i, i ^ distance) for i in range(4)])


def tensor_place():
    mine = lax.axis_index("tensor")
    return mine % 2, mine // 2


def tensor_scatter(partial):
    core, side = tensor_place()
    half = partial.shape[0] // 2
    quarter = half // 2
    other = swap(lax.dynamic_slice_in_dim(partial, (1 - core) * half, half, 0), 1)
    pair = lax.dynamic_slice_in_dim(partial, core * half, half, 0).astype(F32) + other.astype(F32)
    across = swap(lax.dynamic_slice_in_dim(pair, (1 - side) * quarter, quarter, 0).astype(BF16), 2)
    return lax.dynamic_slice_in_dim(pair, side * quarter, quarter, 0) + across.astype(F32)


def ordered(mine, other, first):
    return jnp.concatenate(
        [jnp.where(first, mine, other), jnp.where(first, other, mine)], axis=0
    )


def tensor_gather(quarter):
    core, side = tensor_place()
    half = ordered(quarter, swap(quarter, 2), side == 0)
    return ordered(half, swap(half, 1), core == 0)


def tensor_sum(value):
    value = value + swap(value, 1)
    return value + swap(value, 2)


def quarter_of(value):
    core, side = tensor_place()
    quarter = value.shape[0] // 4
    return lax.dynamic_slice_in_dim(value, (core * 2 + side) * quarter, quarter, 0)


def chain_states(decay, state, backward):
    n = lax.axis_size("dp")

    def shifted(value, distance):
        pairs = [(i, i + distance) for i in range(n - distance)]
        if backward:
            pairs = [(b, a) for a, b in pairs]
        return lax.ppermute(value, "dp", pairs)

    def pack(decay, state):
        return jnp.concatenate([state, jnp.broadcast_to(decay, (16, DK))], axis=0).astype(BF16)

    def unpack(packed):
        packed = packed.astype(F32)
        return packed[DV : DV + 1], packed[:DV]

    decay, state = unpack(shifted(pack(decay, state), 1))
    distance = 1
    while distance < n - 1:
        more_decay, more_state = unpack(shifted(pack(decay, state), distance))
        decay, state = decay * more_decay, decay * more_state + state
        distance *= 2
    return state


def segments(info_ref, places):
    total = jnp.zeros_like(places)
    for j in range(1, info_ref.shape[0]):
        total = total + (info_ref[j] <= places).astype(jnp.int32)
    return total


def block_masks(info_ref, block):
    start = info_ref[0] + block * BLOCK
    rows = lax.broadcasted_iota(jnp.int32, (BLOCK, 1), 0)
    columns = lax.broadcasted_iota(jnp.int32, (1, BLOCK), 1)
    segment = segments(info_ref, start + rows)
    segment_row = segments(info_ref, start + columns)
    allowed = (columns <= rows) & (segment_row == segment)
    previous = segments(info_ref, start - 1)
    last = segments(info_ref, start + BLOCK - 1)
    before = segments(info_ref, info_ref[0] - 1)
    carry = (segment == previous).astype(F32)
    carry_last = (last == previous).astype(F32)
    same_last = (segment == last).astype(F32)
    alive = (segment == before).astype(F32)
    alive_last = (last == before).astype(F32)
    alive_start = (previous == before).astype(F32)
    return allowed, carry, carry_last, same_last, alive, alive_last, alive_start


def triangle(lower, strict):
    rows = lax.broadcasted_iota(jnp.int32, (BLOCK, BLOCK), 0)
    columns = lax.broadcasted_iota(jnp.int32, (BLOCK, BLOCK), 1)
    if not lower:
        rows, columns = columns, rows
    return ((columns < rows) if strict else (columns <= rows)).astype(F32)


def log_decay_of(logit):
    return (jnp.minimum(logit, 0.0) - jnp.log1p(jnp.exp(-jnp.abs(logit)))) / GATE_NORMALIZER


def forward_kernel(
    info_ref, q_ref, k_ref, v_ref, low_ref, up_ref, bias_ref,
    out_ref, reached_ref, logit_ref, scores_ref, states_ref, total_ref, end_ref, reach_ref,
    state, total,
):
    block = pl.program_id(0)

    @pl.when(block == 0)
    def _():
        state[...] = jnp.zeros_like(state)
        total[...] = jnp.zeros_like(total)

    allowed, carry, carry_last, same_last, alive, alive_last, _ = block_masks(info_ref, block)
    q = q_ref[...] * (DK**-0.5)
    k = k_ref[...]
    v = v_ref[...].astype(BF16)
    logit = (
        jnp.dot(low_ref[:, :RANK], up_ref[...], precision=HIGHEST, preferred_element_type=F32)
        + bias_ref[...]
    )
    logit_ref[...] = logit
    decays = jnp.dot(
        triangle(True, False), log_decay_of(logit), precision=HIGHEST, preferred_element_type=F32
    )
    middle = decays[BLOCK // 2 - 1 : BLOCK // 2]
    end = decays[BLOCK - 1 :]
    scores = lax.dot_general(
        q * jnp.exp(decays - middle), k * jnp.exp(middle - decays), (NT, ((), ())),
        precision=HIGHEST, preferred_element_type=F32,
    )
    scores = jnp.where(allowed, scores, 0.0).astype(BF16)
    scores_ref[...] = scores
    held = state[...]
    states_ref[0] = held.astype(BF16)
    total_ref[0] = total[...]
    q_carry = q * jnp.exp(decays) * carry
    out_ref[...] = low_dot(scores, v, NN) + low_dot(q_carry, held, NT)
    k_end = k * jnp.exp(end - decays) * same_last
    state[...] = held * (jnp.exp(end) * carry_last) + low_dot(v, k_end, TN)
    reached_ref[...] = (q * jnp.exp(decays + total[...]) * alive).astype(BF16)
    total[...] = total[...] + end

    @pl.when(block == pl.num_programs(0) - 1)
    def _():
        end_ref[...] = state[...]
        reach_ref[...] = jnp.exp(total[...]) * alive_last


def forward_states(info, mixer, up_rank, bias):
    count = mixer.shape[0]
    blocks = count // BLOCK
    at_block = lambda i, info: (i, 0)
    fixed = lambda i, info: (0, 0)
    return pl.pallas_call(
        forward_kernel,
        grid_spec=pltpu.PrefetchScalarGridSpec(
            num_scalar_prefetch=1,
            grid=(blocks,),
            in_specs=[
                pl.BlockSpec((BLOCK, DK), lambda i, info: (i, 0)),
                pl.BlockSpec((BLOCK, DK), lambda i, info: (i, 1)),
                pl.BlockSpec((BLOCK, DV), lambda i, info: (i, 1)),
                pl.BlockSpec((BLOCK, SMALL), lambda i, info: (i, (2 * DK + DV) // SMALL)),
                pl.BlockSpec((RANK, DK), fixed),
                pl.BlockSpec((1, DK), fixed),
            ],
            out_specs=[
                pl.BlockSpec((BLOCK, DV), at_block),
                pl.BlockSpec((BLOCK, DK), at_block),
                pl.BlockSpec((BLOCK, DK), at_block),
                pl.BlockSpec((BLOCK, BLOCK), at_block),
                pl.BlockSpec((1, DV, DK), lambda i, info: (i, 0, 0)),
                pl.BlockSpec((1, 1, DK), lambda i, info: (i, 0, 0)),
                pl.BlockSpec((DV, DK), fixed),
                pl.BlockSpec((1, DK), fixed),
            ],
            scratch_shapes=[pltpu.VMEM((DV, DK), F32), pltpu.VMEM((1, DK), F32)],
        ),
        out_shape=[
            jax.ShapeDtypeStruct((count, DV), F32),
            jax.ShapeDtypeStruct((count, DK), BF16),
            jax.ShapeDtypeStruct((count, DK), F32),
            jax.ShapeDtypeStruct((count, BLOCK), BF16),
            jax.ShapeDtypeStruct((blocks, DV, DK), BF16),
            jax.ShapeDtypeStruct((blocks, 1, DK), F32),
            jax.ShapeDtypeStruct((DV, DK), F32),
            jax.ShapeDtypeStruct((1, DK), F32),
        ],
        compiler_params=pltpu.CompilerParams(vmem_limit_bytes=VMEM_BYTES),
        cost_estimate=pl.CostEstimate(flops=10**10, bytes_accessed=2 * 10**7, transcendentals=10**6),
        name="forward_states",
    )(info, mixer, mixer, mixer, mixer, up_rank, bias)


def backward_kernel(
    info_ref, q_ref, k_ref, v_ref, low_ref, logit_ref, scores_ref, states_ref, total_ref, grad_ref,
    up_ref, incoming_ref, later_ref,
    out_ref, up_grad_ref, bias_grad_ref,
    adjoint,
):
    step = pl.program_id(0)
    block = pl.num_programs(0) - 1 - step

    @pl.when(step == 0)
    def _():
        adjoint[...] = later_ref[...]
        up_grad_ref[...] = jnp.zeros_like(up_grad_ref)
        bias_grad_ref[...] = jnp.zeros_like(bias_grad_ref)

    allowed, carry, carry_last, same_last, _, _, alive_start = block_masks(info_ref, block)
    q = q_ref[...] * (DK**-0.5)
    k = k_ref[...]
    v = v_ref[...].astype(BF16)
    grad_exact = grad_ref[...]
    grad = grad_exact.astype(BF16)
    grad_rest = (grad_exact - grad.astype(F32)).astype(BF16)
    logit = logit_ref[...]
    decays = jnp.dot(
        triangle(True, False), log_decay_of(logit), precision=HIGHEST, preferred_element_type=F32
    )
    middle = decays[BLOCK // 2 - 1 : BLOCK // 2]
    end = decays[BLOCK - 1 :]
    q_factor = jnp.exp(decays - middle)
    k_factor = jnp.exp(middle - decays)
    carry_factor = jnp.exp(decays) * carry
    end_factor = jnp.exp(end - decays) * same_last
    q_low = (q * q_factor).astype(BF16)
    k_low = (k * k_factor).astype(BF16)
    q_carry = (q * carry_factor).astype(BF16)
    k_end = (k * end_factor).astype(BF16)
    held = states_ref[0].astype(F32) + incoming_ref[...] * (jnp.exp(total_ref[0]) * alive_start)
    after = adjoint[...]
    held_low = held.astype(BF16)
    after_low = after.astype(BF16)
    scores = scores_ref[...]
    d_scores = low_dot(grad, v, NT) + low_dot(grad_rest, v, NT)
    d_scores = jnp.where(allowed, d_scores, 0.0).astype(BF16)
    d_q_low = low_dot(d_scores, k_low, NN)
    d_k_low = low_dot(d_scores, q_low, TN)
    d_v = low_dot(scores, grad, TN) + low_dot(k_end, after_low, NT)
    d_q_carry = low_dot(grad, held_low, NN)
    d_k_end = low_dot(v, after_low, NN)
    d_q = d_q_low * q_factor + d_q_carry * carry_factor
    d_k = d_k_low * k_factor + d_k_end * end_factor
    later_part = (
        d_q_low * q_low.astype(F32)
        - d_k_low * k_low.astype(F32)
        + d_q_carry * q_carry.astype(F32)
    )
    earlier_part = d_k_end * k_end.astype(F32)
    through = jnp.exp(end) * carry_last
    state_part = through * jnp.sum(after * held, axis=0, keepdims=True)
    d_decay = (
        jnp.dot(triangle(False, False), later_part, precision=HIGHEST, preferred_element_type=F32)
        + jnp.dot(triangle(True, True), earlier_part, precision=HIGHEST, preferred_element_type=F32)
        + state_part
    )
    adjoint[...] = after * through + low_dot(grad, q_carry, TN)
    d_logit = d_decay * jax.nn.sigmoid(-logit) * (1.0 / GATE_NORMALIZER)
    low = low_ref[:, :RANK]
    up_grad_ref[...] += lax.dot_general(
        low, d_logit, (TN, ((), ())), precision=HIGHEST, preferred_element_type=F32
    )
    bias_grad_ref[...] += jnp.sum(d_logit, axis=0, keepdims=True)
    d_low = lax.dot_general(
        d_logit, up_ref[...], (NT, ((), ())), precision=HIGHEST, preferred_element_type=F32
    )
    out_ref[:, :DK] = (d_q * (DK**-0.5)).astype(BF16)
    out_ref[:, DK : 2 * DK] = d_k.astype(BF16)
    out_ref[:, 2 * DK : 2 * DK + DV] = d_v.astype(BF16)
    out_ref[:, 2 * DK + DV :] = d_low.astype(BF16)


def backward_states(info, mixer, logit, scores, states, total, grad, up_rank, incoming, later):
    count = mixer.shape[0]
    blocks = count // BLOCK
    width = mixer.shape[1]
    up_wide = jnp.pad(up_rank, ((0, SMALL - RANK), (0, 0)))
    fixed = lambda i, info: (0, 0)
    turned = lambda column: (lambda i, info: (blocks - 1 - i, column))
    turned3 = lambda i, info: (blocks - 1 - i, 0, 0)
    return pl.pallas_call(
        backward_kernel,
        grid_spec=pltpu.PrefetchScalarGridSpec(
            num_scalar_prefetch=1,
            grid=(blocks,),
            in_specs=[
                pl.BlockSpec((BLOCK, DK), turned(0)),
                pl.BlockSpec((BLOCK, DK), turned(1)),
                pl.BlockSpec((BLOCK, DV), turned(1)),
                pl.BlockSpec((BLOCK, SMALL), turned((2 * DK + DV) // SMALL)),
                pl.BlockSpec((BLOCK, DK), turned(0)),
                pl.BlockSpec((BLOCK, BLOCK), turned(0)),
                pl.BlockSpec((1, DV, DK), turned3),
                pl.BlockSpec((1, 1, DK), turned3),
                pl.BlockSpec((BLOCK, DV), turned(0)),
                pl.BlockSpec((SMALL, DK), fixed),
                pl.BlockSpec((DV, DK), fixed),
                pl.BlockSpec((DV, DK), fixed),
            ],
            out_specs=[
                pl.BlockSpec((BLOCK, width), turned(0)),
                pl.BlockSpec((RANK, DK), fixed),
                pl.BlockSpec((1, DK), fixed),
            ],
            scratch_shapes=[pltpu.VMEM((DV, DK), F32)],
        ),
        out_shape=[
            jax.ShapeDtypeStruct((count, width), BF16),
            jax.ShapeDtypeStruct((RANK, DK), F32),
            jax.ShapeDtypeStruct((1, DK), F32),
        ],
        compiler_params=pltpu.CompilerParams(vmem_limit_bytes=VMEM_BYTES),
        cost_estimate=pl.CostEstimate(flops=2 * 10**10, bytes_accessed=2 * 10**7, transcendentals=10**6),
        name="backward_states",
    )(info, mixer, mixer, mixer, mixer, logit, scores, states, total, grad, up_wide, incoming, later)


def head_parts(mixed, outgate, gain):
    inverse = lax.rsqrt(jnp.mean(mixed * mixed, axis=-1, keepdims=True) + EPSILON)
    unit = mixed * inverse
    return inverse, unit, unit * gain, jax.nn.sigmoid(outgate)


def mix_kernel(within_ref, reached_ref, incoming_ref, outgate_ref, gain_ref, weight_ref,
               mixed_ref, gated_ref, branch_ref):
    mixed = within_ref[...] + low_dot(reached_ref[...], incoming_ref[...], NT)
    mixed_ref[...] = mixed
    outgate = outgate_ref[...]
    _, _, head_out, sigmoid = head_parts(mixed, outgate, gain_ref[...])
    gated = (head_out * (outgate * sigmoid)).astype(BF16)
    gated_ref[...] = gated
    branch_ref[...] = low_dot(gated, weight_ref[...], NN).astype(BF16)


def mix(within, reached, incoming, outgate, gain, weight):
    count, width = within.shape[0], weight.shape[1]
    rows = min(256, count)
    at_block = lambda i: (i, 0)
    fixed = lambda i: (0, 0)
    return pl.pallas_call(
        mix_kernel,
        grid=(count // rows,),
        in_specs=[
            pl.BlockSpec((rows, DV), at_block),
            pl.BlockSpec((rows, DK), at_block),
            pl.BlockSpec((DV, DK), fixed),
            pl.BlockSpec((rows, DV), at_block),
            pl.BlockSpec((1, DV), fixed),
            pl.BlockSpec((DV, width), fixed),
        ],
        out_specs=[
            pl.BlockSpec((rows, DV), at_block),
            pl.BlockSpec((rows, DV), at_block),
            pl.BlockSpec((rows, width), at_block),
        ],
        out_shape=[
            jax.ShapeDtypeStruct((count, DV), F32),
            jax.ShapeDtypeStruct((count, DV), BF16),
            jax.ShapeDtypeStruct((count, width), BF16),
        ],
        compiler_params=pltpu.CompilerParams(vmem_limit_bytes=VMEM_BYTES),
        cost_estimate=pl.CostEstimate(flops=6 * 10**9, bytes_accessed=2 * 10**7, transcendentals=10**6),
        name="mix",
    )(within, reached, incoming, outgate, gain, weight)


def unmix_kernel(grad_ref, weight_ref, mixed_ref, outgate_ref, gain_ref, reached_ref,
                 d_mixed_ref, d_outgate_ref, gain_grad_ref, own_ref):
    @pl.when(pl.program_id(0) == 0)
    def _():
        gain_grad_ref[...] = jnp.zeros_like(gain_grad_ref)
        own_ref[...] = jnp.zeros_like(own_ref)

    d_gated = low_dot(grad_ref[...], weight_ref[...], NT)
    outgate = outgate_ref[...]
    gain = gain_ref[...]
    inverse, unit, head_out, sigmoid = head_parts(mixed_ref[...], outgate, gain)
    d_head_out = d_gated * (outgate * sigmoid)
    d_outgate = d_gated * head_out * sigmoid * (1.0 + outgate * (1.0 - sigmoid))
    d_outgate_ref[...] = d_outgate.astype(BF16)
    gain_grad_ref[...] += jnp.sum(d_head_out * unit, axis=0, keepdims=True)
    scaled = d_head_out * gain
    d_mixed = inverse * (scaled - unit * jnp.mean(scaled * unit, axis=-1, keepdims=True))
    d_mixed_ref[...] = d_mixed
    own_ref[...] += low_dot(d_mixed, reached_ref[...], TN)


def unmix(grad, weight, mixed, outgate, gain, reached):
    count, width = grad.shape
    rows = min(256, count)
    at_block = lambda i: (i, 0)
    fixed = lambda i: (0, 0)
    return pl.pallas_call(
        unmix_kernel,
        grid=(count // rows,),
        in_specs=[
            pl.BlockSpec((rows, width), at_block),
            pl.BlockSpec((DV, width), fixed),
            pl.BlockSpec((rows, DV), at_block),
            pl.BlockSpec((rows, DV), at_block),
            pl.BlockSpec((1, DV), fixed),
            pl.BlockSpec((rows, DK), at_block),
        ],
        out_specs=[
            pl.BlockSpec((rows, DV), at_block),
            pl.BlockSpec((rows, DV), at_block),
            pl.BlockSpec((1, DV), fixed),
            pl.BlockSpec((DV, DK), fixed),
        ],
        out_shape=[
            jax.ShapeDtypeStruct((count, DV), F32),
            jax.ShapeDtypeStruct((count, DV), BF16),
            jax.ShapeDtypeStruct((1, DV), F32),
            jax.ShapeDtypeStruct((DV, DK), F32),
        ],
        compiler_params=pltpu.CompilerParams(vmem_limit_bytes=VMEM_BYTES),
        cost_estimate=pl.CostEstimate(flops=6 * 10**9, bytes_accessed=2 * 10**7, transcendentals=10**6),
        name="unmix",
    )(grad, weight, mixed, outgate, gain, reached)


def rms_inverse(values):
    return lax.rsqrt(jnp.mean(values * values, axis=-1, keepdims=True) + EPSILON)


def norm_back(d_normed, gains, unit, inverse):
    scaled = d_normed * gains
    return inverse * (scaled - unit * jnp.mean(scaled * unit, axis=-1, keepdims=True))


def product(left, right):
    return jnp.dot(left, right, preferred_element_type=F32)


def shards(
    tokens, out_grad, starts, attn_gain, w_query, w_key, w_value, w_outgate, w_decay_down,
    w_decay_up, decay_bias, head_gain, w_output, ffn_gain, w_gate, w_up, w_down,
):
    ring = Ring("dp")
    n = ring.n
    rows = w_query.shape[0]
    ranks, heads = w_decay_up.shape[1], head_gain.shape[0]

    side = jnp.zeros((rows, SMALL), BF16)
    side = side.at[:, :RANK].set(w_decay_down)
    side = side.at[:, RANK].set(attn_gain)
    side = side.at[:, RANK + 1].set(ffn_gain)
    side = side.at[:RANK, 32 : 32 + ranks].set(w_decay_up)
    side = side.at[RANK, 32 : 32 + ranks].set(decay_bias)
    side = side.at[RANK + 1, 32 : 32 + heads].set(head_gain)
    mixer_part = jnp.concatenate([w_query, w_key, w_value, side], axis=1)
    width = mixer_part.shape[1]
    half = rows // 2
    halves = ring.gather([mixer_part[:half], mixer_part[half:]], [0, 0])
    full_mixer = jnp.concatenate(
        [h.reshape(n, half, width) for h in halves], axis=1
    ).reshape(n * rows, width)
    full_outgate, full_output = ring.gather([w_outgate, w_output], [0, 1])
    full_gate, full_up = ring.gather([w_gate, w_up], [0, 0])
    (full_down,) = ring.gather([w_down], [1])

    full_side = full_mixer[:, width - SMALL :]
    gain_one = full_side[:, RANK].astype(F32)
    gain_two = full_side[:, RANK + 1].astype(F32)
    blocks = full_side.reshape(n, rows, SMALL)
    up_rank = (
        blocks[:, :RANK, 32 : 32 + ranks].transpose(1, 0, 2).reshape(RANK, n * ranks).astype(F32)
    )
    bias = blocks[:, RANK, 32 : 32 + ranks].reshape(1, n * ranks).astype(F32)
    head_gains = blocks[:, RANK + 1, 32 : 32 + heads].reshape(1, n * heads).astype(F32)

    count = tokens.shape[0]
    info = jnp.concatenate([(lax.axis_index("dp") * count)[None].astype(jnp.int32), starts])

    inputs = tokens.astype(F32)
    normed = (inputs * rms_inverse(inputs) * gain_one).astype(BF16)
    mixer = product(normed, full_mixer)
    within, reached, logit, scores, states, total, end, reach = forward_states(
        info, mixer, up_rank, bias
    )
    incoming = chain_states(reach, end, False)
    outgate = product(normed, full_outgate)
    mixed, gated, branch_part = mix(within, reached, incoming, outgate, head_gains, full_output)
    hidden_in = quarter_of(inputs) + tensor_scatter(branch_part)

    inverse_two = rms_inverse(hidden_in)
    unit_two = hidden_in * inverse_two
    normed_two = tensor_gather((unit_two * gain_two).astype(BF16))
    gate_pre = product(normed_two, full_gate)
    up_proj = product(normed_two, full_up)
    gate_sigmoid = jax.nn.sigmoid(gate_pre)
    gate_silu = gate_pre * gate_sigmoid
    hidden = (gate_silu * up_proj).astype(BF16)
    ffn_out = tensor_scatter(product(hidden, full_down).astype(BF16))
    output = tensor_gather((hidden_in + ffn_out).astype(BF16))

    d_hidden = jnp.einsum("td,fd->tf", out_grad, full_down, preferred_element_type=F32)
    d_gate = (d_hidden * up_proj * gate_sigmoid * (1.0 + gate_pre * (1.0 - gate_sigmoid))).astype(
        BF16
    )
    d_up = (d_hidden * gate_silu).astype(BF16)
    d_normed_part = jnp.einsum("tf,df->td", d_gate, full_gate, preferred_element_type=F32)
    d_normed_part = d_normed_part + jnp.einsum(
        "tf,df->td", d_up, full_up, preferred_element_type=F32
    )
    d_normed_two = tensor_scatter(d_normed_part.astype(BF16))

    def columns_of(value, d):
        return lax.dynamic_slice_in_dim(value, d * rows, rows, 1)

    def rows_maker(left, right):
        return lambda d: jnp.einsum(
            "tr,tc->rc", columns_of(left, d), right, preferred_element_type=F32
        )

    def columns_maker(left, right):
        return lambda d: jnp.einsum(
            "tr,tc->rc", left, columns_of(right, d), preferred_element_type=F32
        )

    (sum_down,) = ring.scatter([columns_maker(hidden, out_grad)])
    sum_gate, sum_up = ring.scatter([rows_maker(normed_two, d_gate), rows_maker(normed_two, d_up)])

    d_hidden_in = quarter_of(out_grad).astype(F32) + norm_back(
        d_normed_two, gain_two, unit_two, inverse_two
    )
    d_branch = tensor_gather(d_hidden_in.astype(BF16))

    d_mixed, d_outgate, grad_head_gain, own = unmix(
        d_branch, full_output, mixed, outgate, head_gains, reached
    )
    later = chain_states(reach, own, True)
    sum_output, sum_outgate = ring.scatter(
        [columns_maker(gated, d_branch), rows_maker(normed, d_outgate)]
    )
    d_mixer, grad_up_rank, grad_bias = backward_states(
        info, mixer, logit, scores, states, total, d_mixed, up_rank, incoming, later
    )
    d_first = jnp.einsum("tk,dk->td", d_mixer, full_mixer, preferred_element_type=F32)
    d_first = d_first + jnp.einsum(
        "tk,dk->td", d_outgate, full_outgate, preferred_element_type=F32
    )
    d_normed = tensor_scatter(d_first.astype(BF16))

    packed = jnp.zeros((n, rows, SMALL), F32)
    packed = packed.at[:, :RANK, 32 : 32 + ranks].set(
        grad_up_rank.reshape(RANK, n, ranks).transpose(1, 0, 2)
    )
    packed = packed.at[:, RANK, 32 : 32 + ranks].set(grad_bias.reshape(n, ranks))
    packed = packed.at[:, RANK + 1, 32 : 32 + heads].set(grad_head_gain.reshape(n, heads))
    packed = packed.reshape(n * rows, SMALL)

    def mixer_maker(upper):
        def maker(d):
            columns = lax.dynamic_slice_in_dim(normed, d * rows + (0 if upper else half), half, 1)
            chunk = jnp.einsum("tr,tc->rc", columns, d_mixer, preferred_element_type=F32)
            extra = lax.dynamic_slice_in_dim(packed, d * rows + (0 if upper else half), half, 0)
            return chunk + jnp.pad(extra, ((0, 0), (width - SMALL, 0)))

        return maker

    sum_mixer = jnp.concatenate(ring.scatter([mixer_maker(True), mixer_maker(False)]), axis=0)
    sum_query, sum_key = sum_mixer[:, :DK], sum_mixer[:, DK : 2 * DK]
    sum_value = sum_mixer[:, 2 * DK : 2 * DK + DV]
    sum_side = sum_mixer[:, 2 * DK + DV :]

    own_inputs = quarter_of(inputs)
    inverse_one = rms_inverse(own_inputs)
    input_grad = tensor_gather(
        (
            d_hidden_in + norm_back(d_normed, gain_one, own_inputs * inverse_one, inverse_one)
        ).astype(BF16)
    ).astype(F32)

    def weighted(pairs):
        return sum(jnp.sum(w.astype(F32) * g, axis=1, keepdims=True) for w, g in pairs)

    attn_part = weighted(
        [
            (w_query, sum_query),
            (w_key, sum_key),
            (w_value, sum_value),
            (w_outgate, sum_outgate),
            (w_decay_down, sum_side[:, :RANK]),
        ]
    )
    ffn_part = weighted([(w_gate, sum_gate), (w_up, sum_up)])
    shared = tensor_sum(jnp.concatenate([sum_side[:, :RANK], attn_part, ffn_part], axis=1))
    return (
        output,
        input_grad,
        shared[:, RANK] / attn_gain.astype(F32),
        sum_query,
        sum_key,
        sum_value,
        sum_outgate,
        shared[:, :RANK],
        sum_side[:RANK, 32 : 32 + ranks],
        sum_side[RANK, 32 : 32 + ranks],
        sum_side[RANK + 1, 32 : 32 + heads],
        sum_output,
        shared[:, RANK + 1] / ffn_gain.astype(F32),
        sum_gate,
        sum_up,
        sum_down,
    )


def solution(mesh):
    return jax.shard_map(
        shards,
        mesh=mesh,
        in_specs=(
            P("dp", None),
            P("dp", None),
            P(),
            P("dp"),
            P("dp", "tensor"),
            P("dp", "tensor"),
            P("dp", "tensor"),
            P("dp", "tensor"),
            P("dp", None),
            P(None, ("tensor", "dp")),
            P(("tensor", "dp")),
            P(("tensor", "dp")),
            P("tensor", "dp"),
            P("dp"),
            P("dp", "tensor"),
            P("dp", "tensor"),
            P("tensor", "dp"),
        ),
        out_specs=(
            P("dp", None),
            P("dp", None),
            P("dp"),
            P("dp", "tensor"),
            P("dp", "tensor"),
            P("dp", "tensor"),
            P("dp", "tensor"),
            P("dp", None),
            P(None, ("tensor", "dp")),
            P(("tensor", "dp")),
            P(("tensor", "dp")),
            P("tensor", "dp"),
            P("dp"),
            P("dp", "tensor"),
            P("dp", "tensor"),
            P("tensor", "dp"),
        ),
        check_vma=False,
    )
```
